32 devices in a mesh: lon: 4 (over z), lat: 2 (over x), mem: 4 (over y, core).
Axes of the slice: x: 2, y: 2, z: 4, core: 2. Of those that a mesh axis runs over, the one named last changes fastest.
Arguments:
- perturb: float32 [8, 2, 2048, 1024], P('mem', None, 'lat', 'lon'), may hold values from -6 to 6
- control: float32 [8, 2, 2048, 1024], P('mem', None, 'lat', 'lon'), may hold values from -6 to 6
- diffusivity: float32 [2048, 1024], P('lat', 'lon'), may hold values from 0.05 to 0.24
- sea_mask: int32 [2, 2048, 1024], P(None, 'lat', 'lon'), may hold values 0 or 1
- fold_partner: int32 [1024], replicated, may hold values from 0 to 1023, as said below
Outputs:
- increment: float32 [2, 2048, 1024], P(None, 'lat', 'lon')
The draws below stay inside these ranges and needn't reach their ends.
Inputs may be any that keep to these rules, and one draw needn't show every extreme that they name: `sea_mask`: 1 marks sea and 0 land. fold_partner[i] = (2 p - 1 - i) mod 1024 for a fold pivot column p of the case; it is its own inverse and never maps a column to itself.
All inputs are finite; a program needn't handle non-finite values. No bound on the sum of `sea_mask` on one device may be relied on, other than what follows from the above.
Results may differ from the reference program's by a relative error of at most 0.00002.
Values sent between devices are 32-bit elements; how exact they have to be, the bound alone decides.
A program may use at most 192 MiB of HBM per device.

```python
import math
import jax
import jax.numpy as jnp
from jax import lax

LEV = 2
PASSES = 3
MEMBERS = 8
LON = 1024
LAT = 2048


def draw_fold_partner(key, part):
    key = jax.random.fold_in(key, 11)
    fold_pivot = jax.random.randint(key, (), 0, LON, dtype=jnp.int32)
    col_ids = jnp.arange(LON, dtype=jnp.int32)
    return jnp.mod(2 * fold_pivot - 1 - col_ids, LON).astype(jnp.int32)


def plant(values, stream_key, smallest, largest):
    longest = values.shape.index(max(values.shape))
    spots = []
    for shift in (0, 1):
        where = [jax.random.randint(jax.random.fold_in(stream_key, axis), (), 0, length) for axis, length in enumerate(values.shape)]
        where[longest] = (where[longest] + shift) % values.shape[longest]
        spots.append(tuple(where))
    return values.at[spots[0]].set(smallest).at[spots[1]].set(largest)


def shard_levels(key, shape, cuts, least, largest):
    def one(dim, shards_of):
        draws = jax.random.uniform(jax.random.fold_in(jax.random.fold_in(key, 6), dim), (shards_of,), jnp.float32, least / len(cuts), largest / len(cuts))
        return jnp.repeat(jnp.exp(draws), shape[dim] // shards_of).reshape((-1,) + (1,) * (len(shape) - dim - 1))

    gain = one(*cuts[0])
    for cut in cuts[1:]:
        gain = gain * one(*cut)
    return gain


def gaussian(key, shape, scale, limit, cuts=(), kind=jnp.bfloat16):
    gain = shard_levels(key, shape, cuts, -0.22, 0.18) if cuts else 1.0
    drawn = jax.random.normal(key, shape, jnp.float32) * scale * gain
    return jnp.minimum(jnp.maximum(drawn, -limit), limit).astype(kind)


def setup_inputs(seed: int = 0) -> dict:
    key_list = jax.random.split(jax.random.key(seed), 6)
    return {
        "perturb": gaussian(key_list[0], (MEMBERS, LEV, LAT, LON), 1.0, 6.0, ((0, 4), (2, 2), (3, 4)), jnp.float32),
        "control": gaussian(key_list[1], (MEMBERS, LEV, LAT, LON), 1.0, 6.0, ((0, 4), (2, 2), (3, 4)), jnp.float32),
        "diffusivity": jnp.clip(jnp.exp(math.log(0.24) - 1.5686159 * jax.random.uniform(key_list[2], (LAT, LON), jnp.float32) ** shard_levels(key_list[2], (LAT, LON), ((0, 2), (1, 4)), -0.2, 0.2)), 0.05, 0.24),
        "sea_mask": plant((jax.random.randint(key_list[3], (LEV, LAT, LON), 0, 10) < 7).astype(jnp.int32), jax.random.fold_in(key_list[3], 1), 0, 1),
        "fold_partner": draw_fold_partner(jax.random.fold_in(key_list[5], 71), 0),
    }


def extend(values, fold_partner):
    north_row = jnp.take(values[..., -1:, :], fold_partner, axis=-1)
    south_row = jnp.zeros_like(values[..., :1, :])
    stacked = jnp.concatenate([south_row, values, north_row], axis=-2)
    return jnp.concatenate([stacked[..., -1:], stacked, stacked[..., :1]], axis=-1)


def diffuse(current, kappa_pad, sea_pad):
    inner_rows = current.shape[-2] - 2
    inner_cols = current.shape[-1] - 2
    centre = current[..., 1:-1, 1:-1]
    kappa_mid = kappa_pad[1:-1, 1:-1]
    sea_mid = sea_pad[..., 1:-1, 1:-1]
    change = jnp.zeros_like(centre)
    for row_off, col_off in ((1, 2), (1, 0), (2, 1), (0, 1)):
        nearby = current[..., row_off:row_off + inner_rows, col_off:col_off + inner_cols]
        kappa_near = kappa_pad[row_off:row_off + inner_rows, col_off:col_off + inner_cols]
        sea_near = sea_pad[..., row_off:row_off + inner_rows, col_off:col_off + inner_cols]
        conduct = 0.5 * (kappa_mid + kappa_near) * sea_mid * sea_near
        change = change + conduct * (nearby - centre)
    return centre + change


def reference(perturb, control, diffusivity, sea_mask, fold_partner):
    sea_float = sea_mask.astype(jnp.float32)
    kappa_pad = extend(diffusivity, fold_partner)
    sea_pad = extend(sea_float, fold_partner)

    def member(running, member_pair):
        spread_field, weights_field = member_pair
        smooth = weights_field
        for sweep in range(PASSES):
            smooth = diffuse(extend(smooth, fold_partner), kappa_pad, sea_pad)
        return running + spread_field * smooth, None

    start = jnp.zeros((LEV, LAT, LON), jnp.float32)
    summed, unused = lax.scan(member, start, (perturb, control))
    return summed * sea_float
```

```python
import functools
import jax
import jax.numpy as jnp
from jax import lax
from jax.experimental import pallas as pl
from jax.experimental.pallas import tpu as pltpu
from jax.sharding import PartitionSpec as P

PASSES = 3
CHUNK = 128
PIECE = 256
MESH = pl.DeviceIdType.MESH


def kernel(
    control, perturb, kappa, sea, side_f, side_i, rim_f, rim_i, out,
    field, weight, kap, mask, g_east, g_north, state,
    part, part_in, pair, pair_in, total,
    in_sem, halo_sem, a_send, a_recv, b_send, b_recv, c_send, c_recv, o_sem,
):
    rows = control.shape[1]
    cols = control.shape[2]
    wide = cols + 128
    blocks = rows // 8
    chunks = rows // CHUNK
    pieces = rows // PIECE
    per_chunk = CHUNK // 8
    mem = lax.axis_index("mem")
    core = lax.rem(mem, 2)
    twin = {"mem": mem + 1 - 2 * core}
    across = {"mem": lax.rem(mem + 2, 4)}

    def piece_copies(p):
        src = pl.ds(pl.multiple_of(p * PIECE, PIECE), PIECE)
        dst = pl.ds(pl.multiple_of(p * PIECE + 8, 8), PIECE)
        return (
            pltpu.make_async_copy(kappa.at[src], kap.at[dst, 0:cols], in_sem.at[0, p]),
            pltpu.make_async_copy(sea.at[:, src], mask.at[:, dst, 0:cols], in_sem.at[1, p]),
            pltpu.make_async_copy(control.at[:, src], field.at[:, dst, 0:cols], in_sem.at[2, p]),
            pltpu.make_async_copy(perturb.at[:, src], weight.at[:, src], in_sem.at[3, p]),
        )

    low = pl.ds(0, 8)
    high = pl.ds(rows + 8, 8)
    main = pl.ds(0, cols)
    side = pl.ds(cols, 128)
    halo_copies = [
        pltpu.make_async_copy(side_f.at[0:4], field.at[:, :, side], halo_sem.at[0]),
        pltpu.make_async_copy(side_f.at[4], kap.at[:, side], halo_sem.at[1]),
        pltpu.make_async_copy(side_i, mask.at[:, :, side], halo_sem.at[2]),
        pltpu.make_async_copy(rim_f.at[0, 0:4], field.at[:, low, main], halo_sem.at[3]),
        pltpu.make_async_copy(rim_f.at[0, 4], kap.at[low, main], halo_sem.at[4]),
        pltpu.make_async_copy(rim_i.at[0], mask.at[:, low, main], halo_sem.at[5]),
        pltpu.make_async_copy(rim_f.at[1, 0:4], field.at[:, high, main], halo_sem.at[6]),
        pltpu.make_async_copy(rim_f.at[1, 4], kap.at[high, main], halo_sem.at[7]),
        pltpu.make_async_copy(rim_i.at[1], mask.at[:, high, main], halo_sem.at[8]),
    ]
    for copy in halo_copies:
        copy.start()
    for copy in piece_copies(0):
        copy.start()

    barrier = pltpu.get_barrier_semaphore()
    for peer in (twin, across):
        pl.semaphore_signal(barrier, inc=1, device_id=peer, device_id_type=MESH)
    pl.semaphore_wait(barrier, 2)

    for p in range(1, pieces):
        for copy in piece_copies(p):
            copy.start()
    for copy in halo_copies:
        copy.wait()
    for copy in piece_copies(0):
        copy.wait()

    row_id = lax.broadcasted_iota(jnp.int32, (8, wide), 0)
    first = row_id == 0
    last = row_id == 7

    def block(idx):
        return pl.ds(pl.multiple_of(idx * 8, 8), 8)

    def apply(cur, nxt, flux_before, ge, gn):
        north = gn * (pltpu.roll(jnp.where(first, nxt, cur), 7, 0) - cur)
        south = pltpu.roll(jnp.where(last, flux_before, north), 1, 0)
        east = ge * (pltpu.roll(cur, wide - 1, 1) - cur)
        west = pltpu.roll(east, 1, 1)
        return cur + ((east - west) + (north - south)), north

    def step(o, carry, level):
        here = jnp.minimum(o + 5, blocks + 1)
        ahead = jnp.minimum(o + 6, blocks + 1)
        second = jnp.minimum(jnp.maximum(o + 3, 0), blocks + 1)
        third = jnp.maximum(o + 1, 0)
        k_here = kap[block(here)]
        s_here = mask[level, block(here)].astype(jnp.float32)
        k_ahead = kap[block(ahead)]
        s_ahead = mask[level, block(ahead)].astype(jnp.float32)
        k_north = pltpu.roll(jnp.where(first, k_ahead, k_here), 7, 0)
        s_north = pltpu.roll(jnp.where(first, s_ahead, s_here), 7, 0)
        k_east = pltpu.roll(k_here, wide - 1, 1)
        s_east = pltpu.roll(s_here, wide - 1, 1)
        half = 0.5 * s_here
        gn1 = (k_here + k_north) * (half * s_north)
        ge1 = (k_here + k_east) * (half * s_east)
        g_north[level, block(here)] = gn1
        g_east[level, block(here)] = ge1
        gn2 = g_north[level, block(second)]
        ge2 = g_east[level, block(second)]
        gn3 = g_north[level, block(third)]
        ge3 = g_east[level, block(third)]
        after = []
        results = []
        for member in range(2):
            v0, f1, n1, c1, f2, n2, c2, f3 = carry[8 * member : 8 * member + 8]
            nxt = field[2 * member + level, block(ahead)]
            w1, f1 = apply(v0, nxt, f1, ge1, gn1)
            w2, f2 = apply(c1, n1, f2, ge2, gn2)
            w3, f3 = apply(c2, n2, f3, ge3, gn3)
            after += [nxt, f1, w1, n1, f2, w2, n2, f3]
            results.append(w3)
        return tuple(after), results

    for level in range(2):
        state[level] = jnp.zeros((16, 8, wide), jnp.float32)
        for member in range(2):
            state[level, 8 * member] = field[2 * member + level, 0:8]
        start = [state[level, i] for i in range(16)]
        warm = lax.fori_loop(-5, 0, lambda o, c: step(o, c, level)[0], tuple(start))
        for i, value in enumerate(warm):
            state[level, i] = value

    def diffuse_chunk(k, level, into):
        def body(j, carry):
            o = k * per_chunk + j
            carry, results = step(o, carry, level)
            acc = weight[level, block(o)] * results[0][:, 0:cols]
            acc = acc + weight[2 + level, block(o)] * results[1][:, 0:cols]
            into[k, block(j)] = acc
            return carry

        carry = tuple(state[level, i] for i in range(16))
        carry = lax.fori_loop(0, per_chunk, body, carry)
        for i, value in enumerate(carry):
            state[level, i] = value

    def send_part(k):
        return pltpu.make_async_remote_copy(
            src_ref=part.at[k], dst_ref=part_in.at[k], send_sem=a_send.at[k],
            recv_sem=a_recv.at[k], device_id=twin, device_id_type=MESH,
        )

    def send_pair(k):
        return pltpu.make_async_remote_copy(
            src_ref=pair.at[k], dst_ref=pair_in.at[k], send_sem=b_send.at[k],
            recv_sem=b_recv.at[k], device_id=across, device_id_type=MESH,
        )

    def chunk_rows(k):
        return pl.ds(pl.multiple_of(k * CHUNK, CHUNK), CHUNK)

    def send_total(k):
        return pltpu.make_async_remote_copy(
            src_ref=total.at[k], dst_ref=out.at[core, chunk_rows(k)], send_sem=c_send.at[k],
            recv_sem=c_recv.at[k], device_id=twin, device_id_type=MESH,
        )

    def store_total(k):
        return pltpu.make_async_copy(total.at[k], out.at[core, chunk_rows(k)], o_sem.at[k])

    ratio = PIECE // CHUNK

    @pl.loop(0, chunks)
    def _(k):
        @pl.when(jnp.logical_and(lax.rem(k, ratio) == ratio - 1, k < chunks - 1))
        def _():
            for copy in piece_copies(lax.div(k, ratio) + 1):
                copy.wait()

        diffuse_chunk(k, 1 - core, part)
        send_part(k).start()
        diffuse_chunk(k, core, pair)
        send_part(k).wait_recv()

        @pl.loop(0, per_chunk)
        def _(j):
            pair[k, block(j)] = pair[k, block(j)] + part_in[k, block(j)]

        send_pair(k).start()

    @pl.loop(0, chunks)
    def _(k):
        send_pair(k).wait_recv()

        @pl.loop(0, per_chunk)
        def _(j):
            sea_here = mask[core, block(k * per_chunk + j + 1), 0:cols].astype(jnp.float32)
            total[k, block(j)] = (pair[k, block(j)] + pair_in[k, block(j)]) * sea_here

        send_total(k).start()
        store_total(k).start()

    @pl.loop(0, chunks)
    def _(k):
        send_part(k).wait_send()
        send_pair(k).wait_send()
        send_total(k).wait()
        store_total(k).wait()


def shifted(block, axis, by):
    count = lax.axis_size(axis)
    return lax.ppermute(block, axis, [(i, (i + by) % count) for i in range(count)])


def per_device(perturb, control, diffusivity, sea_mask, fold_partner):
    members, levels, rows, cols = control.shape
    fields = members * levels
    flat = control.reshape(fields, rows, cols)
    sea_float = lambda s: s.astype(jnp.float32)
    lon = lax.axis_index("lon")
    lat = lax.axis_index("lat")
    top_band = lat == lax.axis_size("lat") - 1
    bottom_band = lat == 0

    def cut(r, c):
        return jnp.concatenate(
            [flat[:, r, c], diffusivity[None, r, c], sea_float(sea_mask[:, r, c])], axis=0
        )

    every = slice(None)
    north_edge = cut(slice(rows - PASSES, rows), every)
    south_edge = cut(slice(0, PASSES), every)
    from_north = shifted(south_edge, "lat", -1)
    from_south = shifted(north_edge, "lat", 1)
    gathered = lax.all_gather(north_edge, "lon", axis=2, tiled=True)
    count = gathered.shape[-1]
    flipped = gathered[:, ::-1, ::-1]
    twice = jnp.concatenate([flipped, flipped], axis=-1)
    begin = jnp.mod(count - 1 - fold_partner[0] + lon * cols, count)
    folded = lax.dynamic_slice_in_dim(twice, begin, cols, axis=2)
    north = jnp.where(top_band, folded, from_north)
    south = jnp.where(bottom_band, jnp.zeros_like(from_south), from_south)

    def strip(c):
        tall = jnp.concatenate([south[:, :, c], cut(every, c), north[:, :, c]], axis=1)
        return jnp.swapaxes(tall, 1, 2)

    from_east = shifted(strip(slice(0, PASSES)), "lon", -1)
    from_west = shifted(strip(slice(cols - PASSES, cols)), "lon", 1)
    gap = 128 - 2 * PASSES
    middle = jnp.zeros((fields + 3, gap, rows + 2 * PASSES), jnp.float32)
    side = jnp.swapaxes(jnp.concatenate([from_east, middle, from_west], axis=1), 1, 2)
    fill = 8 - PASSES
    side = jnp.pad(side, ((0, 0), (fill, fill), (0, 0)))
    rim = jnp.stack(
        [
            jnp.pad(south, ((0, 0), (fill, 0), (0, 0))),
            jnp.pad(north, ((0, 0), (0, fill), (0, 0))),
        ]
    )
    chunks = rows // CHUNK
    wide = cols + 128
    any_spec = pl.BlockSpec(memory_space=pl.ANY)
    f32 = jnp.float32
    chunk_buf = pltpu.VMEM((chunks, CHUNK, cols), f32)
    dma = pltpu.SemaphoreType.DMA
    return pl.pallas_call(
        kernel,
        out_shape=jax.ShapeDtypeStruct((levels, rows, cols), f32),
        in_specs=[any_spec] * 8,
        out_specs=any_spec,
        scratch_shapes=[
            pltpu.VMEM((fields, rows + 16, wide), f32),
            pltpu.VMEM((fields, rows, cols), f32),
            pltpu.VMEM((rows + 16, wide), f32),
            pltpu.VMEM((levels, rows + 16, wide), jnp.int32),
            pltpu.VMEM((levels, rows + 16, wide), f32),
            pltpu.VMEM((levels, rows + 16, wide), f32),
            pltpu.VMEM((levels, 16, 8, wide), f32),
            chunk_buf, chunk_buf, chunk_buf, chunk_buf, chunk_buf,
            dma((4, rows // PIECE)),
            dma((9,)),
            dma((chunks,)), dma((chunks,)), dma((chunks,)), dma((chunks,)),
            dma((chunks,)), dma((chunks,)), dma((chunks,)),
        ],
        compiler_params=pltpu.CompilerParams(
            collective_id=0, has_side_effects=True, vmem_limit_bytes=50 * 1024 * 1024
        ),
        cost_estimate=pl.CostEstimate(
            flops=40 * fields * rows * cols, bytes_accessed=16 * fields * rows * cols, transcendentals=0
        ),
    )(
        flat,
        perturb.reshape(fields, rows, cols),
        diffusivity,
        sea_mask,
        side[: fields + 1],
        side[fields + 1 :].astype(jnp.int32),
        rim[:, : fields + 1],
        rim[:, fields + 1 :].astype(jnp.int32),
    )


def solution(mesh):
    return jax.shard_map(
        per_device,
        mesh=mesh,
        in_specs=(
            P("mem", None, "lat", "lon"),
            P("mem", None, "lat", "lon"),
            P("lat", "lon"),
            P(None, "lat", "lon"),
            P(),
        ),
        out_specs=P(None, "lat", "lon"),
        check_vma=False,
    )
```

```python
import jax
import jax.numpy as jnp
from jax import lax
from jax.experimental import pallas as pl
from jax.experimental.pallas import tpu as pltpu
from jax.sharding import PartitionSpec as P

PASSES = 3
CHUNK = 128
STEP = 4
PAD = 4
LEAD = 10
TAIL = 16
MESH = pl.DeviceIdType.MESH


def kernel(
    control, perturb, kappa, sea, pivot, out,
    field, once, again, weight, kap, mask, sea_int, g_east, g_north, state,
    pack, pack_in, top, top_in,
    part, part_in, pair, pair_in, total,
    in_sem, side_send, side_recv, rim_send, rim_recv, top_send, top_recv,
    a_send, a_recv, b_send, b_recv, c_send, c_recv, o_sem,
):
    fields, rows, cols = control.shape
    levels = fields // 2
    wide = cols + 128
    blocks = rows // 8
    chunks = rows // CHUNK
    per_chunk = CHUNK // 8
    count = lax.axis_size("lon")
    lon = lax.axis_index("lon")
    lat = lax.axis_index("lat")
    mem = lax.axis_index("mem")
    core = lax.rem(mem, 2)
    twin = {"mem": mem + 1 - 2 * core}
    across = {"mem": lax.rem(mem + 2, 4)}
    facing = {"lat": 1 - lat}
    lon_peer = [None] + [{"lon": lax.rem(lon + d, count)} for d in range(1, count)]
    east_peer = lon_peer[1]
    west_peer = lon_peer[count - 1]
    bottom_band = lat == 0
    top_band = lat == 1

    body_rows = pl.ds(PAD * 8, rows)
    loads = [
        pltpu.make_async_copy(control, field.at[:, body_rows, 0:cols], in_sem.at[0]),
        pltpu.make_async_copy(kappa, kap.at[body_rows, 0:cols], in_sem.at[1]),
        pltpu.make_async_copy(sea, sea_int, in_sem.at[2]),
        pltpu.make_async_copy(perturb, weight, in_sem.at[3]),
    ]
    for copy in loads:
        copy.start()

    barrier = pltpu.get_barrier_semaphore()
    peers = lon_peer[1:] + [facing, twin, across]
    for peer in peers:
        pl.semaphore_signal(barrier, inc=1, device_id=peer, device_id_type=MESH)
    for copy in loads[:3]:
        copy.wait()

    row_id = lax.broadcasted_iota(jnp.int32, (8, wide), 0)
    first = row_id == 0
    last = row_id == 7
    lane = lax.broadcasted_iota(jnp.int32, (8, 128), 1)

    def block(idx):
        return pl.ds(pl.multiple_of((idx + PAD) * 8, 8), 8)

    def plain(idx):
        return pl.ds(pl.multiple_of(idx * 8, 8), 8)

    def source(item, idx, c):
        if item < fields:
            return field[item, block(idx), c]
        if item == fields:
            return kap[block(idx), c]
        return mask[item - fields - 1, block(idx), c]

    def store(item, idx, c, value):
        if item < fields:
            field[item, block(idx), c] = value
        elif item == fields:
            kap[block(idx), c] = value
        else:
            mask[item - fields - 1, block(idx), c] = value

    items = fields + 1 + levels
    groups = 4
    quarter = blocks // groups
    slot_of = lambda item, g: g * (128 // groups) + item * PASSES
    left = slice(0, 128)
    right = slice(cols - 128, cols)
    extra = slice(cols, wide)

    @pl.loop(0, quarter)
    def _(b):
        west = jnp.zeros((8, 128), jnp.float32)
        east = jnp.zeros((8, 128), jnp.float32)
        for g in range(groups):
            idx = g * quarter + b
            for lev in range(levels):
                mask[lev, block(idx), 0:cols] = sea_int[lev, plain(idx)].astype(jnp.float32)
            for item in range(items):
                slot = slot_of(item, g)
                here = jnp.logical_and(lane >= slot, lane < slot + PASSES)
                if item <= fields:
                    lo = source(item, idx, left)
                    hi = source(item, idx, right)
                else:
                    lo = sea_int[item - fields - 1, plain(idx), left].astype(jnp.float32)
                    hi = sea_int[item - fields - 1, plain(idx), right].astype(jnp.float32)
                if slot:
                    lo = pltpu.roll(lo, slot, 1)
                west = jnp.where(here, lo, west)
                east = jnp.where(here, pltpu.roll(hi, slot + PASSES, 1), east)
        pack[0, plain(b)] = west
        pack[1, plain(b)] = east

    for item in range(items):
        top[item] = source(item, blocks - 1, slice(0, cols))

    pl.semaphore_wait(barrier, len(peers))

    def side_copy(way, peer):
        return pltpu.make_async_remote_copy(
            src_ref=pack.at[way], dst_ref=pack_in.at[way], send_sem=side_send.at[way],
            recv_sem=side_recv.at[way], device_id=peer, device_id_type=MESH,
        )

    sides = [side_copy(0, west_peer), side_copy(1, east_peer)]
    for copy in sides:
        copy.start()
    gathers = [
        pltpu.make_async_remote_copy(
            src_ref=top, dst_ref=top_in.at[d - 1], send_sem=top_send.at[d - 1],
            recv_sem=top_recv.at[d - 1], device_id=lon_peer[d], device_id_type=MESH,
        )
        for d in range(1, count)
    ]
    for copy in gathers:
        copy.start()
    for copy in sides:
        copy.wait_recv()

    @pl.loop(0, quarter)
    def _(b):
        from_east = pack_in[0, plain(b)]
        from_west = pack_in[1, plain(b)]
        for g in range(groups):
            for item in range(items):
                slot = slot_of(item, g)
                near = pltpu.roll(from_east, 128 - slot, 1) if slot else from_east
                far = pltpu.roll(from_west, 128 - slot - PASSES, 1)
                store(item, g * quarter + b, extra, jnp.where(lane < 64, near, far))

    rim_from = block((blocks - 1) * (1 - lat))
    rim_to = block(lat * (blocks + 1) - 1)
    rims = [
        pltpu.make_async_remote_copy(
            src_ref=src, dst_ref=dst, send_sem=rim_send.at[i], recv_sem=rim_recv.at[i],
            device_id=facing, device_id_type=MESH,
        )
        for i, (src, dst) in enumerate((
            (field.at[:, rim_from], field.at[:, rim_to]),
            (kap.at[rim_from], kap.at[rim_to]),
            (mask.at[:, rim_from], mask.at[:, rim_to]),
        ))
    ]
    for copy in rims:
        copy.start()

    @pl.when(bottom_band)
    def _():
        for item in range(items):
            store(item, -1, slice(0, wide), jnp.zeros((8, wide), jnp.float32))

    loads[3].wait()
    for copy in rims:
        copy.wait_recv()

    def fold():
        lanes = lax.broadcasted_iota(jnp.int32, (cols, wide), 1)
        offset = lax.broadcasted_iota(jnp.int32, (cols, wide), 0)
        span = count * cols
        column = lon * cols + jnp.where(lanes < cols + 64, lanes, lanes - wide)
        aim = pivot[0] - column - offset
        acc = jnp.zeros((items * 8, wide), jnp.float32)
        for d in range(count):
            origin = lax.rem(lon + count - d, count) * cols
            gap = aim - origin
            hit = gap == 0
            for turn in (span, -span, -2 * span):
                hit = jnp.logical_or(hit, gap == turn)
            held = top[...] if d == 0 else top_in[d - 1]
            acc = acc + lax.dot_general(
                held.reshape(items * 8, cols), jnp.where(hit, 1.0, 0.0),
                (((1,), (0,)), ((), ())), precision=lax.Precision.HIGHEST,
                preferred_element_type=jnp.float32,
            )
        for item in range(items):
            rows8 = acc[item * 8 : item * 8 + 8]
            ghost = jnp.where(
                first, pltpu.roll(rows8, 1, 0),
                jnp.where(row_id == 1, pltpu.roll(rows8, 3, 0), pltpu.roll(rows8, 5, 0)),
            )
            store(item, blocks, slice(0, wide), ghost)

    def up(cur, nxt):
        return pltpu.roll(jnp.where(first, nxt, cur), 7, 0)

    def sweep(origin, gauges, before):
        results = []
        for i in range(STEP):
            cur = origin[i]
            ge, gn = gauges[i]
            north = gn * (up(cur, origin[i + 1]) - cur)
            south = pltpu.roll(jnp.where(last, before, north), 1, 0)
            east = ge * (pltpu.roll(cur, wide - 1, 1) - cur)
            west = pltpu.roll(east, 1, 1)
            results.append(cur + ((east - west) + (north - south)))
            before = north
        return results, before

    def advance(level, a, depth, emit=None):
        held = [[state[level, m, p] for p in range(depth)] for m in range(2)]
        for p in range(depth - 1, -1, -1):
            at = a - 5 * p
            origin_ref = (field, once, again)[p]
            gauges = [
                (g_east[level, block(at + i)], g_north[level, block(at + i)]) for i in range(STEP)
            ]
            finals = []
            for m in range(2):
                n = levels * m + level
                origin = [origin_ref[n, block(at + i)] for i in range(STEP + 1)]
                results, held[m][p] = sweep(origin, gauges, held[m][p])
                if p < 2:
                    for i in range(STEP):
                        (once, again)[p][n, block(at + i)] = results[i]
                finals.append(results)
            if p == 2 and emit is not None:
                emit(finals)
        for m in range(2):
            for p in range(depth):
                state[level, m, p] = held[m][p]
        at = a + STEP
        ks = [kap[block(at + i)] for i in range(STEP + 1)]
        ss = [mask[level, block(at + i)] for i in range(STEP + 1)]
        for i in range(STEP):
            half = 0.5 * ss[i]
            g_north[level, block(at + i)] = (ks[i] + up(ks[i], ks[i + 1])) * (
                half * up(ss[i], ss[i + 1])
            )
            g_east[level, block(at + i)] = (ks[i] + pltpu.roll(ks[i], wide - 1, 1)) * (
                half * pltpu.roll(ss[i], wide - 1, 1)
            )

    @pl.loop(0, levels)
    def _(level):
        for depth in range(4):
            advance(level, LEAD - TAIL + STEP * depth, depth)

    def diffuse_chunk(k, level, into):
        @pl.loop(0, per_chunk // STEP)
        def _(j):
            o = k * per_chunk + j * STEP

            def emit(finals):
                for i in range(STEP):
                    acc = weight[level, plain(o + i)] * finals[0][i][:, 0:cols]
                    acc = acc + weight[levels + level, plain(o + i)] * finals[1][i][:, 0:cols]
                    into[k, plain(j * STEP + i)] = acc

            advance(level, o + LEAD, 3, emit)

    def send_part(k):
        return pltpu.make_async_remote_copy(
            src_ref=part.at[k], dst_ref=part_in.at[k], send_sem=a_send.at[k],
            recv_sem=a_recv.at[k], device_id=twin, device_id_type=MESH,
        )

    def send_pair(k):
        return pltpu.make_async_remote_copy(
            src_ref=pair.at[k], dst_ref=pair_in.at[k], send_sem=b_send.at[k],
            recv_sem=b_recv.at[k], device_id=across, device_id_type=MESH,
        )

    def chunk_rows(k):
        return pl.ds(pl.multiple_of(k * CHUNK, CHUNK), CHUNK)

    def send_total(k):
        return pltpu.make_async_remote_copy(
            src_ref=total.at[k], dst_ref=out.at[core, chunk_rows(k)], send_sem=c_send.at[k],
            recv_sem=c_recv.at[k], device_id=twin, device_id_type=MESH,
        )

    def store_total(k):
        return pltpu.make_async_copy(total.at[k], out.at[core, chunk_rows(k)], o_sem.at[k])

    @pl.loop(0, chunks)
    def _(k):
        @pl.when(k == chunks - 2)
        def _():
            for copy in gathers:
                copy.wait_recv()

            @pl.when(top_band)
            def _():
                fold()

        diffuse_chunk(k, 1 - core, part)
        send_part(k).start()
        diffuse_chunk(k, core, pair)
        send_part(k).wait_recv()

        @pl.loop(0, per_chunk)
        def _(j):
            pair[k, plain(j)] = pair[k, plain(j)] + part_in[k, plain(j)]

        send_pair(k).start()

    @pl.loop(0, chunks)
    def _(k):
        send_pair(k).wait_recv()

        @pl.loop(0, per_chunk)
        def _(j):
            sea_here = mask[core, block(k * per_chunk + j), 0:cols]
            total[k, plain(j)] = (pair[k, plain(j)] + pair_in[k, plain(j)]) * sea_here

        send_total(k).start()
        store_total(k).start()

    @pl.loop(0, chunks)
    def _(k):
        send_part(k).wait_send()
        send_pair(k).wait_send()
        send_total(k).wait()
        store_total(k).wait()

    for copy in sides + gathers + rims:
        copy.wait_send()


def per_device(perturb, control, diffusivity, sea_mask, fold_partner):
    members, levels, rows, cols = control.shape
    fields = members * levels
    chunks = rows // CHUNK
    wide = cols + 128
    tall = rows + 8 * (PAD + TAIL)
    items = fields + 1 + levels
    count = lax.axis_size("lon")
    f32 = jnp.float32
    any_spec = pl.BlockSpec(memory_space=pl.ANY)
    chunk_buf = pltpu.VMEM((chunks, CHUNK, cols), f32)
    full = pltpu.VMEM((fields, tall, wide), f32)
    by_level = pltpu.VMEM((levels, tall, wide), f32)
    packed = pltpu.VMEM((2, rows // 4, 128), f32)
    dma = pltpu.SemaphoreType.DMA
    return pl.pallas_call(
        kernel,
        out_shape=jax.ShapeDtypeStruct((levels, rows, cols), f32),
        in_specs=[any_spec] * 4 + [pl.BlockSpec(memory_space=pltpu.SMEM)],
        out_specs=any_spec,
        scratch_shapes=[
            full, full, full,
            pltpu.VMEM((fields, rows, cols), f32),
            pltpu.VMEM((tall, wide), f32),
            by_level,
            pltpu.VMEM((levels, rows, cols), jnp.int32),
            by_level, by_level,
            pltpu.VMEM((levels, members, PASSES, 8, wide), f32),
            packed, packed,
            pltpu.VMEM((items, 8, cols), f32),
            pltpu.VMEM((count - 1, items, 8, cols), f32),
            chunk_buf, chunk_buf, chunk_buf, chunk_buf, chunk_buf,
            dma((4,)), dma((2,)), dma((2,)), dma((3,)), dma((3,)),
            dma((count - 1,)), dma((count - 1,)),
            dma((chunks,)), dma((chunks,)), dma((chunks,)), dma((chunks,)),
            dma((chunks,)), dma((chunks,)), dma((chunks,)),
        ],
        compiler_params=pltpu.CompilerParams(
            collective_id=0, has_side_effects=True, vmem_limit_bytes=60 * 1024 * 1024
        ),
        cost_estimate=pl.CostEstimate(
            flops=40 * fields * rows * cols, bytes_accessed=16 * fields * rows * cols, transcendentals=0
        ),
    )(
        control.reshape(fields, rows, cols),
        perturb.reshape(fields, rows, cols),
        diffusivity,
        sea_mask,
        fold_partner[:1],
    )


def solution(mesh):
    return jax.shard_map(
        per_device,
        mesh=mesh,
        in_specs=(
            P("mem", None, "lat", "lon"),
            P("mem", None, "lat", "lon"),
            P("lat", "lon"),
            P(None, "lat", "lon"),
            P(),
        ),
        out_specs=P(None, "lat", "lon"),
        check_vma=False,
    )
```

```python
import jax
import jax.numpy as jnp
from jax import lax
from jax.experimental import pallas as pl
from jax.experimental.pallas import tpu as pltpu
from jax.sharding import PartitionSpec as P

PASSES = 3
CHUNK = 128
STEP = 4
PAD = 4
LEAD = 10
TAIL = 16
LANES = 128
MESH = pl.DeviceIdType.MESH


def kernel(
    control, perturb, kappa, sea, pivot, out,
    field, once, again, weight, kap, mask, sea_int, g_mid, g_east, g_west, g_north,
    pack, pack_in, top, top_in,
    part, part_in, pair, pair_in, total,
    in_sem, side_send, side_recv, rim_send, rim_recv, top_send, top_recv,
    a_send, a_recv, b_send, b_recv, c_send, c_recv, o_sem,
):
    fields, rows, cols = control.shape
    levels = fields // 2
    tiles = cols // LANES
    wide = cols + LANES
    blocks = rows // 8
    chunks = rows // CHUNK
    per_chunk = CHUNK // 8
    count = lax.axis_size("lon")
    lon = lax.axis_index("lon")
    lat = lax.axis_index("lat")
    mem = lax.axis_index("mem")
    core = lax.rem(mem, 2)
    twin = {"mem": mem + 1 - 2 * core}
    across = {"mem": lax.rem(mem + 2, 4)}
    facing = {"lat": 1 - lat}
    lon_peer = [None] + [{"lon": lax.rem(lon + d, count)} for d in range(1, count)]
    east_peer = lon_peer[1]
    west_peer = lon_peer[count - 1]
    bottom_band = lat == 0
    top_band = lat == 1

    body_rows = pl.ds(PAD * 8, rows)
    loads = [
        pltpu.make_async_copy(sea, sea_int, in_sem.at[0]),
        pltpu.make_async_copy(perturb, weight, in_sem.at[1]),
    ]
    for t in range(tiles):
        span = slice(t * LANES, (t + 1) * LANES)
        loads += [
            pltpu.make_async_copy(control.at[:, :, span], field.at[:, t, body_rows], in_sem.at[2 + 2 * t]),
            pltpu.make_async_copy(kappa.at[:, span], kap.at[t, body_rows], in_sem.at[3 + 2 * t]),
        ]
    for copy in loads:
        copy.start()

    barrier = pltpu.get_barrier_semaphore()
    peers = lon_peer[1:] + [facing, twin, across]
    for peer in peers:
        pl.semaphore_signal(barrier, inc=1, device_id=peer, device_id_type=MESH)
    for copy in loads[:1] + loads[2:]:
        copy.wait()

    row_id = lax.broadcasted_iota(jnp.int32, (8, wide), 0)
    first = row_id == 0
    lane = lax.broadcasted_iota(jnp.int32, (8, 128), 1)

    def block(idx, by=0):
        return pl.ds(pl.multiple_of((idx + PAD) * 8, 8) + by, 8)

    def plain(idx):
        return pl.ds(pl.multiple_of(idx * 8, 8), 8)

    def source(item, idx, t):
        if item < fields:
            return field[item, t, block(idx)]
        if item == fields:
            return kap[t, block(idx)]
        return mask[item - fields - 1, t, block(idx)]

    def store(item, idx, t, value):
        if item < fields:
            field[item, t, block(idx)] = value
        elif item == fields:
            kap[t, block(idx)] = value
        else:
            mask[item - fields - 1, t, block(idx)] = value

    items = fields + 1 + levels
    groups = 4
    quarter = blocks // groups
    slot_of = lambda item, g: g * (128 // groups) + item * PASSES
    left = 0
    right = tiles - 1

    @pl.loop(0, quarter)
    def _(b):
        west = jnp.zeros((8, 128), jnp.float32)
        east = jnp.zeros((8, 128), jnp.float32)
        for g in range(groups):
            idx = g * quarter + b
            for lev in range(levels):
                for t in range(tiles):
                    span = slice(t * LANES, (t + 1) * LANES)
                    mask[lev, t, block(idx)] = sea_int[lev, plain(idx), span].astype(jnp.float32)
            for item in range(items):
                slot = slot_of(item, g)
                here = jnp.logical_and(lane >= slot, lane < slot + PASSES)
                if item <= fields:
                    lo = source(item, idx, left)
                    hi = source(item, idx, right)
                else:
                    lo = sea_int[item - fields - 1, plain(idx), 0:LANES].astype(jnp.float32)
                    hi = sea_int[item - fields - 1, plain(idx), cols - LANES : cols].astype(jnp.float32)
                if slot:
                    lo = pltpu.roll(lo, slot, 1)
                west = jnp.where(here, lo, west)
                east = jnp.where(here, pltpu.roll(hi, slot + PASSES, 1), east)
        pack[0, plain(b)] = west
        pack[1, plain(b)] = east

    for item in range(items):
        for t in range(tiles):
            top[item, :, t * LANES : (t + 1) * LANES] = source(item, blocks - 1, t)

    pl.semaphore_wait(barrier, len(peers))

    def side_copy(way, peer):
        return pltpu.make_async_remote_copy(
            src_ref=pack.at[way], dst_ref=pack_in.at[way], send_sem=side_send.at[way],
            recv_sem=side_recv.at[way], device_id=peer, device_id_type=MESH,
        )

    sides = [side_copy(0, west_peer), side_copy(1, east_peer)]
    for copy in sides:
        copy.start()
    gathers = [
        pltpu.make_async_remote_copy(
            src_ref=top, dst_ref=top_in.at[d - 1], send_sem=top_send.at[d - 1],
            recv_sem=top_recv.at[d - 1], device_id=lon_peer[d], device_id_type=MESH,
        )
        for d in range(1, count)
    ]
    for copy in gathers:
        copy.start()
    for copy in sides:
        copy.wait_recv()

    @pl.loop(0, quarter)
    def _(b):
        from_east = pack_in[0, plain(b)]
        from_west = pack_in[1, plain(b)]
        for g in range(groups):
            for item in range(items):
                slot = slot_of(item, g)
                near = pltpu.roll(from_east, 128 - slot, 1) if slot else from_east
                far = pltpu.roll(from_west, 128 - slot - PASSES, 1)
                store(item, g * quarter + b, tiles, jnp.where(lane < 64, near, far))

    rim_from = block((blocks - 1) * (1 - lat))
    rim_to = block(lat * (blocks + 1) - 1)
    rims = [
        pltpu.make_async_remote_copy(
            src_ref=src, dst_ref=dst, send_sem=rim_send.at[i], recv_sem=rim_recv.at[i],
            device_id=facing, device_id_type=MESH,
        )
        for i, (src, dst) in enumerate((
            (field.at[:, :, rim_from], field.at[:, :, rim_to]),
            (kap.at[:, rim_from], kap.at[:, rim_to]),
            (mask.at[:, :, rim_from], mask.at[:, :, rim_to]),
        ))
    ]
    for copy in rims:
        copy.start()

    @pl.when(bottom_band)
    def _():
        for item in range(items):
            for t in range(tiles + 1):
                store(item, -1, t, jnp.zeros((8, LANES), jnp.float32))

    loads[1].wait()
    for copy in rims:
        copy.wait_recv()

    def fold():
        lanes = lax.broadcasted_iota(jnp.int32, (cols, wide), 1)
        offset = lax.broadcasted_iota(jnp.int32, (cols, wide), 0)
        span = count * cols
        column = lon * cols + jnp.where(lanes < cols + 64, lanes, lanes - wide)
        aim = pivot[0] - column - offset
        acc = jnp.zeros((items * 8, wide), jnp.float32)
        for d in range(count):
            origin = lax.rem(lon + count - d, count) * cols
            gap = aim - origin
            hit = gap == 0
            for turn in (span, -span, -2 * span):
                hit = jnp.logical_or(hit, gap == turn)
            held = top[...] if d == 0 else top_in[d - 1]
            acc = acc + lax.dot_general(
                held.reshape(items * 8, cols), jnp.where(hit, 1.0, 0.0),
                (((1,), (0,)), ((), ())), precision=lax.Precision.HIGHEST,
                preferred_element_type=jnp.float32,
            )
        for item in range(items):
            rows8 = acc[item * 8 : item * 8 + 8]
            ghost = jnp.where(
                first, pltpu.roll(rows8, 1, 0),
                jnp.where(row_id == 1, pltpu.roll(rows8, 3, 0), pltpu.roll(rows8, 5, 0)),
            )
            for t in range(tiles + 1):
                store(item, blocks, t, ghost[:, t * LANES : (t + 1) * LANES])

    lane_first = lane == 0
    lane_last = lane == LANES - 1

    def eastward(values):
        turned = [pltpu.roll(v, LANES - 1, 1) for v in values]
        return [
            jnp.where(lane_last, turned[(t + 1) % len(values)], turned[t])
            for t in range(len(values))
        ]

    def westward(values):
        turned = [pltpu.roll(v, 1, 1) for v in values]
        return [jnp.where(lane_first, turned[t - 1], turned[t]) for t in range(len(values))]

    every = range(tiles + 1)

    def advance(level, a, depth, emit=None):
        for p in range(depth - 1, -1, -1):
            origin = (field, once, again)[p]
            for i in range(STEP):
                at = a - 5 * p + i
                used = range(tiles) if p == 2 else every
                gains = [
                    (
                        g_mid[level, t, block(at)], g_east[level, t, block(at)],
                        g_west[level, t, block(at)], g_north[level, t, block(at)],
                        g_north[level, t, block(at, -1)],
                    )
                    for t in used
                ]
                finals = []
                for m in range(2):
                    n = levels * m + level
                    cur = [origin[n, t, block(at)] for t in every]
                    east = eastward(cur)
                    west = westward(cur)
                    for t in used:
                        gm, ge, gw, gn, gs = gains[t]
                        value = (gm * cur[t] + (ge * east[t] + gw * west[t])) + (
                            gn * origin[n, t, block(at, 1)] + gs * origin[n, t, block(at, -1)]
                        )
                        if p < 2:
                            (once, again)[p][n, t, block(at)] = value
                        else:
                            finals.append(value)
                if p == 2:
                    emit(i, finals)
        for i in range(STEP):
            at = a + STEP + i
            ks = [kap[t, block(at)] for t in every]
            ss = [mask[level, t, block(at)] for t in every]
            k_east, s_east = eastward(ks), eastward(ss)
            k_west, s_west = westward(ks), westward(ss)
            for t in every:
                half = 0.5 * ss[t]
                ge = (ks[t] + k_east[t]) * (half * s_east[t])
                gw = (ks[t] + k_west[t]) * (half * s_west[t])
                gn = (ks[t] + kap[t, block(at, 1)]) * (half * mask[level, t, block(at, 1)])
                gs = (ks[t] + kap[t, block(at, -1)]) * (half * mask[level, t, block(at, -1)])
                g_mid[level, t, block(at)] = 1.0 - ((ge + gw) + (gn + gs))
                g_east[level, t, block(at)] = ge
                g_west[level, t, block(at)] = gw
                g_north[level, t, block(at)] = gn

    @pl.loop(0, levels)
    def _(level):
        for turn, depth in enumerate((0, 1, 2, 2)):
            advance(level, LEAD - TAIL + STEP * turn, depth)

    def diffuse_chunk(k, level, into):
        @pl.loop(0, per_chunk // STEP)
        def _(j):
            o = k * per_chunk + j * STEP

            def emit(i, finals):
                for t in range(tiles):
                    span = slice(t * LANES, (t + 1) * LANES)
                    acc = weight[level, plain(o + i), span] * finals[t]
                    acc = acc + weight[levels + level, plain(o + i), span] * finals[tiles + t]
                    into[k, plain(j * STEP + i), span] = acc

            advance(level, o + LEAD, 3, emit)

    def send_part(k):
        return pltpu.make_async_remote_copy(
            src_ref=part.at[k], dst_ref=part_in.at[k], send_sem=a_send.at[k],
            recv_sem=a_recv.at[k], device_id=twin, device_id_type=MESH,
        )

    def send_pair(k):
        return pltpu.make_async_remote_copy(
            src_ref=pair.at[k], dst_ref=pair_in.at[k], send_sem=b_send.at[k],
            recv_sem=b_recv.at[k], device_id=across, device_id_type=MESH,
        )

    def chunk_rows(k):
        return pl.ds(pl.multiple_of(k * CHUNK, CHUNK), CHUNK)

    def send_total(k):
        return pltpu.make_async_remote_copy(
            src_ref=total.at[k], dst_ref=out.at[core, chunk_rows(k)], send_sem=c_send.at[k],
            recv_sem=c_recv.at[k], device_id=twin, device_id_type=MESH,
        )

    def store_total(k):
        return pltpu.make_async_copy(total.at[k], out.at[core, chunk_rows(k)], o_sem.at[k])

    @pl.loop(0, chunks)
    def _(k):
        @pl.when(k == chunks - 2)
        def _():
            for copy in gathers:
                copy.wait_recv()

            @pl.when(top_band)
            def _():
                fold()

        diffuse_chunk(k, 1 - core, part)
        send_part(k).start()
        diffuse_chunk(k, core, pair)
        send_part(k).wait_recv()

        @pl.loop(0, per_chunk)
        def _(j):
            pair[k, plain(j)] = pair[k, plain(j)] + part_in[k, plain(j)]

        send_pair(k).start()

    @pl.loop(0, chunks)
    def _(k):
        send_pair(k).wait_recv()

        @pl.loop(0, per_chunk)
        def _(j):
            for t in range(tiles):
                span = slice(t * LANES, (t + 1) * LANES)
                total[k, plain(j), span] = (
                    pair[k, plain(j), span] + pair_in[k, plain(j), span]
                ) * mask[core, t, block(k * per_chunk + j)]

        send_total(k).start()
        store_total(k).start()

    @pl.loop(0, chunks)
    def _(k):
        send_part(k).wait_send()
        send_pair(k).wait_send()
        send_total(k).wait()
        store_total(k).wait()

    for copy in sides + gathers + rims:
        copy.wait_send()


def per_device(perturb, control, diffusivity, sea_mask, fold_partner):
    members, levels, rows, cols = control.shape
    fields = members * levels
    chunks = rows // CHUNK
    span = cols // LANES + 1
    tall = rows + 8 * (PAD + TAIL)
    items = fields + 1 + levels
    count = lax.axis_size("lon")
    f32 = jnp.float32
    any_spec = pl.BlockSpec(memory_space=pl.ANY)
    chunk_buf = pltpu.VMEM((chunks, CHUNK, cols), f32)
    full = pltpu.VMEM((fields, span, tall, LANES), f32)
    by_level = pltpu.VMEM((levels, span, tall, LANES), f32)
    packed = pltpu.VMEM((2, rows // 4, 128), f32)
    dma = pltpu.SemaphoreType.DMA
    return pl.pallas_call(
        kernel,
        out_shape=jax.ShapeDtypeStruct((levels, rows, cols), f32),
        in_specs=[any_spec] * 4 + [pl.BlockSpec(memory_space=pltpu.SMEM)],
        out_specs=any_spec,
        scratch_shapes=[
            full, full, full,
            pltpu.VMEM((fields, rows, cols), f32),
            pltpu.VMEM((span, tall, LANES), f32),
            by_level,
            pltpu.VMEM((levels, rows, cols), jnp.int32),
            by_level, by_level, by_level, by_level,
            packed, packed,
            pltpu.VMEM((items, 8, cols), f32),
            pltpu.VMEM((count - 1, items, 8, cols), f32),
            chunk_buf, chunk_buf, chunk_buf, chunk_buf, chunk_buf,
            dma((2 * span,)), dma((2,)), dma((2,)), dma((3,)), dma((3,)),
            dma((count - 1,)), dma((count - 1,)),
            dma((chunks,)), dma((chunks,)), dma((chunks,)), dma((chunks,)),
            dma((chunks,)), dma((chunks,)), dma((chunks,)),
        ],
        compiler_params=pltpu.CompilerParams(
            collective_id=0, has_side_effects=True, vmem_limit_bytes=60 * 1024 * 1024
        ),
        cost_estimate=pl.CostEstimate(
            flops=40 * fields * rows * cols, bytes_accessed=16 * fields * rows * cols, transcendentals=0
        ),
    )(
        control.reshape(fields, rows, cols),
        perturb.reshape(fields, rows, cols),
        diffusivity,
        sea_mask,
        fold_partner[:1],
    )


def solution(mesh):
    return jax.shard_map(
        per_device,
        mesh=mesh,
        in_specs=(
            P("mem", None, "lat", "lon"),
            P("mem", None, "lat", "lon"),
            P("lat", "lon"),
            P(None, "lat", "lon"),
            P(),
        ),
        out_specs=P(None, "lat", "lon"),
        check_vma=False,
    )
```

```python
import jax
import jax.numpy as jnp
from jax import lax
from jax.experimental import pallas as pl
from jax.experimental.pallas import tpu as pltpu
from jax.sharding import PartitionSpec as P

PASSES = 3
CHUNK = 128
STEP = 4
PAD = 4
LEAD = 10
TAIL = 16
LANES = 128
MESH = pl.DeviceIdType.MESH


def kernel(
    control, perturb, kappa, sea, pivot, out,
    field, once, again, weight, kap, mask, sea_int, g_mid, g_east, g_west, g_north,
    pack, pack_in, top, top_in,
    part, part_in, pair, pair_in, total,
    in_sem, side_send, side_recv, rim_send, rim_recv, top_send, top_recv,
    a_send, a_recv, b_send, b_recv, c_send, c_recv, o_sem,
):
    fields, rows, cols = control.shape
    levels = fields // 2
    tiles = cols // LANES
    wide = cols + LANES
    blocks = rows // 8
    chunks = rows // CHUNK
    per_chunk = CHUNK // 8
    count = lax.axis_size("lon")
    lon = lax.axis_index("lon")
    lat = lax.axis_index("lat")
    mem = lax.axis_index("mem")
    core = lax.rem(mem, 2)
    twin = {"mem": mem + 1 - 2 * core}
    across = {"mem": lax.rem(mem + 2, 4)}
    facing = {"lat": 1 - lat}
    lon_peer = [None] + [{"lon": lax.rem(lon + d, count)} for d in range(1, count)]
    east_peer = lon_peer[1]
    west_peer = lon_peer[count - 1]
    bottom_band = lat == 0
    top_band = lat == 1

    body_rows = pl.ds(PAD * 8, rows)
    loads = [
        pltpu.make_async_copy(sea, sea_int, in_sem.at[0]),
        pltpu.make_async_copy(perturb, weight, in_sem.at[1]),
    ]
    for t in range(tiles):
        span = slice(t * LANES, (t + 1) * LANES)
        loads += [
            pltpu.make_async_copy(control.at[:, :, span], field.at[:, t, body_rows], in_sem.at[2 + 2 * t]),
            pltpu.make_async_copy(kappa.at[:, span], kap.at[t, body_rows], in_sem.at[3 + 2 * t]),
        ]
    for copy in loads[:1] + loads[2:]:
        copy.start()

    barrier = pltpu.get_barrier_semaphore()
    peers = lon_peer[1:] + [facing, twin, across]
    for peer in peers:
        pl.semaphore_signal(barrier, inc=1, device_id=peer, device_id_type=MESH)
    for copy in loads[:1] + loads[2:]:
        copy.wait()

    row_id = lax.broadcasted_iota(jnp.int32, (8, wide), 0)
    first = row_id == 0
    lane = lax.broadcasted_iota(jnp.int32, (8, 128), 1)

    def block(idx, by=0):
        return pl.ds(pl.multiple_of((idx + PAD) * 8, 8) + by, 8)

    def plain(idx):
        return pl.ds(pl.multiple_of(idx * 8, 8), 8)

    def source(item, idx, t):
        if item < fields:
            return field[item, t, block(idx)]
        if item == fields:
            return kap[t, block(idx)]
        return mask[item - fields - 1, t, block(idx)]

    def store(item, idx, t, value):
        if item < fields:
            field[item, t, block(idx)] = value
        elif item == fields:
            kap[t, block(idx)] = value
        else:
            mask[item - fields - 1, t, block(idx)] = value

    items = fields + 1 + levels
    groups = 4
    quarter = blocks // groups
    slot_of = lambda item, g: g * (128 // groups) + item * PASSES
    left = 0
    right = tiles - 1

    loads[1].start()
    part_blocks = quarter // 2
    starts = (0, 1, 2, 7), (3, 4, 5, 6)

    def pack_part(h):
      @pl.loop(0, part_blocks)
      def _(b):
        west = jnp.zeros((8, 128), jnp.float32)
        east = jnp.zeros((8, 128), jnp.float32)
        for g in range(groups):
            idx = starts[h][g] * part_blocks + b
            for lev in range(levels):
                for t in range(tiles):
                    span = slice(t * LANES, (t + 1) * LANES)
                    mask[lev, t, block(idx)] = sea_int[lev, plain(idx), span].astype(jnp.float32)
            for item in range(items):
                slot = slot_of(item, g)
                here = jnp.logical_and(lane >= slot, lane < slot + PASSES)
                if item <= fields:
                    lo = source(item, idx, left)
                    hi = source(item, idx, right)
                else:
                    lo = sea_int[item - fields - 1, plain(idx), 0:LANES].astype(jnp.float32)
                    hi = sea_int[item - fields - 1, plain(idx), cols - LANES : cols].astype(jnp.float32)
                if slot:
                    lo = pltpu.roll(lo, slot, 1)
                west = jnp.where(here, lo, west)
                east = jnp.where(here, pltpu.roll(hi, slot + PASSES, 1), east)
        pack[0, plain(h * part_blocks + b)] = west
        pack[1, plain(h * part_blocks + b)] = east

    pack_part(0)
    pl.semaphore_wait(barrier, len(peers))

    def side_copy(way, h, peer):
        span = pl.ds(h * part_blocks * 8, part_blocks * 8)
        sem = 2 * h + way
        return pltpu.make_async_remote_copy(
            src_ref=pack.at[way, span], dst_ref=pack_in.at[way, span], send_sem=side_send.at[sem],
            recv_sem=side_recv.at[sem], device_id=peer, device_id_type=MESH,
        )

    halves = [[side_copy(0, h, west_peer), side_copy(1, h, east_peer)] for h in range(2)]
    sides = halves[0] + halves[1]
    for copy in halves[0]:
        copy.start()
    pack_part(1)
    for copy in halves[1]:
        copy.start()
    for item in range(items):
        for t in range(tiles):
            top[item, :, t * LANES : (t + 1) * LANES] = source(item, blocks - 1, t)

    gathers = [
        pltpu.make_async_remote_copy(
            src_ref=top, dst_ref=top_in.at[d - 1], send_sem=top_send.at[d - 1],
            recv_sem=top_recv.at[d - 1], device_id=lon_peer[d], device_id_type=MESH,
        )
        for d in range(1, count)
    ]
    for copy in gathers:
        copy.start()

    def unpack_part(h):
      for copy in halves[h]:
        copy.wait_recv()

      @pl.loop(0, part_blocks)
      def _(b):
        from_east = pack_in[0, plain(h * part_blocks + b)]
        from_west = pack_in[1, plain(h * part_blocks + b)]
        for g in range(groups):
            for item in range(items):
                slot = slot_of(item, g)
                near = pltpu.roll(from_east, 128 - slot, 1) if slot else from_east
                far = pltpu.roll(from_west, 128 - slot - PASSES, 1)
                store(item, starts[h][g] * part_blocks + b, tiles, jnp.where(lane < 64, near, far))

    unpack_part(0)
    rim_from = block((blocks - 1) * (1 - lat))
    rim_to = block(lat * (blocks + 1) - 1)
    rims = [
        pltpu.make_async_remote_copy(
            src_ref=src, dst_ref=dst, send_sem=rim_send.at[i], recv_sem=rim_recv.at[i],
            device_id=facing, device_id_type=MESH,
        )
        for i, (src, dst) in enumerate((
            (field.at[:, :, rim_from], field.at[:, :, rim_to]),
            (kap.at[:, rim_from], kap.at[:, rim_to]),
            (mask.at[:, :, rim_from], mask.at[:, :, rim_to]),
        ))
    ]
    for copy in rims:
        copy.start()

    @pl.when(bottom_band)
    def _():
        for item in range(items):
            for t in range(tiles + 1):
                store(item, -1, t, jnp.zeros((8, LANES), jnp.float32))

    loads[1].wait()
    for copy in rims:
        copy.wait_recv()

    def fold():
        lanes = lax.broadcasted_iota(jnp.int32, (cols, wide), 1)
        offset = lax.broadcasted_iota(jnp.int32, (cols, wide), 0)
        span = count * cols
        column = lon * cols + jnp.where(lanes < cols + 64, lanes, lanes - wide)
        aim = pivot[0] - column - offset
        acc = jnp.zeros((items * 8, wide), jnp.float32)
        for d in range(count):
            origin = lax.rem(lon + count - d, count) * cols
            gap = aim - origin
            hit = gap == 0
            for turn in (span, -span, -2 * span):
                hit = jnp.logical_or(hit, gap == turn)
            held = top[...] if d == 0 else top_in[d - 1]
            acc = acc + lax.dot_general(
                held.reshape(items * 8, cols), jnp.where(hit, 1.0, 0.0),
                (((1,), (0,)), ((), ())), precision=lax.Precision.HIGHEST,
                preferred_element_type=jnp.float32,
            )
        for item in range(items):
            rows8 = acc[item * 8 : item * 8 + 8]
            ghost = jnp.where(
                first, pltpu.roll(rows8, 1, 0),
                jnp.where(row_id == 1, pltpu.roll(rows8, 3, 0), pltpu.roll(rows8, 5, 0)),
            )
            for t in range(tiles + 1):
                store(item, blocks, t, ghost[:, t * LANES : (t + 1) * LANES])

    lane_first = lane == 0
    lane_last = lane == LANES - 1

    def eastward(values):
        turned = [pltpu.roll(v, LANES - 1, 1) for v in values]
        return [
            jnp.where(lane_last, turned[(t + 1) % len(values)], turned[t])
            for t in range(len(values))
        ]

    def westward(values):
        turned = [pltpu.roll(v, 1, 1) for v in values]
        return [jnp.where(lane_first, turned[t - 1], turned[t]) for t in range(len(values))]

    every = range(tiles + 1)

    def advance(level, a, depth, emit=None, put=None):
        for p in range(depth - 1, -1, -1):
            origin = (field, once, again)[p]
            made = []
            for i in range(STEP):
                at = a - 5 * p + i
                used = range(tiles) if p == 2 else every
                gains = [
                    (
                        g_mid[level, t, block(at)], g_east[level, t, block(at)],
                        g_west[level, t, block(at)], g_north[level, t, block(at)],
                        g_north[level, t, block(at, -1)],
                    )
                    for t in used
                ]
                finals = []
                for m in range(2):
                    n = levels * m + level
                    cur = [origin[n, t, block(at)] for t in every]
                    east = eastward(cur)
                    west = westward(cur)
                    for t in used:
                        gm, ge, gw, gn, gs = gains[t]
                        value = (gm * cur[t] + (ge * east[t] + gw * west[t])) + (
                            gn * origin[n, t, block(at, 1)] + gs * origin[n, t, block(at, -1)]
                        )
                        if p < 2:
                            made.append((n, t, at, value))
                        else:
                            finals.append(value)
                if p == 2:
                    made.append((i, emit(i, finals)))
            for entry in made:
                if p == 2:
                    put(*entry)
                else:
                    n, t, at, value = entry
                    (once, again)[p][n, t, block(at)] = value
        made = []
        for i in range(STEP):
            at = a + STEP + i
            ks = [kap[t, block(at)] for t in every]
            ss = [mask[level, t, block(at)] for t in every]
            k_east, s_east = eastward(ks), eastward(ss)
            k_west, s_west = westward(ks), westward(ss)
            for t in every:
                half = 0.5 * ss[t]
                ge = (ks[t] + k_east[t]) * (half * s_east[t])
                gw = (ks[t] + k_west[t]) * (half * s_west[t])
                gn = (ks[t] + kap[t, block(at, 1)]) * (half * mask[level, t, block(at, 1)])
                gs = (ks[t] + kap[t, block(at, -1)]) * (half * mask[level, t, block(at, -1)])
                made.append((t, at, 1.0 - ((ge + gw) + (gn + gs)), ge, gw, gn))
        for t, at, gm, ge, gw, gn in made:
            g_mid[level, t, block(at)] = gm
            g_east[level, t, block(at)] = ge
            g_west[level, t, block(at)] = gw
            g_north[level, t, block(at)] = gn

    @pl.loop(0, levels)
    def _(level):
        for turn, depth in enumerate((0, 1, 2, 2)):
            advance(level, LEAD - TAIL + STEP * turn, depth)

    def diffuse_chunk(k, level, into):
        @pl.loop(0, per_chunk // STEP)
        def _(j):
            o = k * per_chunk + j * STEP

            def emit(i, finals):
                sums = []
                for t in range(tiles):
                    span = slice(t * LANES, (t + 1) * LANES)
                    acc = weight[level, plain(o + i), span] * finals[t]
                    sums.append(acc + weight[levels + level, plain(o + i), span] * finals[tiles + t])
                return sums

            def put(i, sums):
                for t in range(tiles):
                    into[k, plain(j * STEP + i), t * LANES : (t + 1) * LANES] = sums[t]

            advance(level, o + LEAD, 3, emit, put)

    def send_part(k):
        return pltpu.make_async_remote_copy(
            src_ref=part.at[k], dst_ref=part_in.at[k], send_sem=a_send.at[k],
            recv_sem=a_recv.at[k], device_id=twin, device_id_type=MESH,
        )

    def send_pair(k):
        return pltpu.make_async_remote_copy(
            src_ref=pair.at[k], dst_ref=pair_in.at[k], send_sem=b_send.at[k],
            recv_sem=b_recv.at[k], device_id=across, device_id_type=MESH,
        )

    def chunk_rows(k):
        return pl.ds(pl.multiple_of(k * CHUNK, CHUNK), CHUNK)

    def send_total(k):
        return pltpu.make_async_remote_copy(
            src_ref=total.at[k], dst_ref=out.at[core, chunk_rows(k)], send_sem=c_send.at[k],
            recv_sem=c_recv.at[k], device_id=twin, device_id_type=MESH,
        )

    def store_total(k):
        return pltpu.make_async_copy(total.at[k], out.at[core, chunk_rows(k)], o_sem.at[k])

    @pl.loop(0, chunks)
    def _(k):
        @pl.when(k == 2)
        def _():
            unpack_part(1)

        @pl.when(k == chunks - 2)
        def _():
            for copy in gathers:
                copy.wait_recv()

            @pl.when(top_band)
            def _():
                fold()

        diffuse_chunk(k, 1 - core, part)
        send_part(k).start()
        diffuse_chunk(k, core, pair)
        send_part(k).wait_recv()

        @pl.loop(0, per_chunk)
        def _(j):
            pair[k, plain(j)] = pair[k, plain(j)] + part_in[k, plain(j)]

        send_pair(k).start()

    @pl.loop(0, chunks)
    def _(k):
        send_pair(k).wait_recv()

        @pl.loop(0, per_chunk)
        def _(j):
            for t in range(tiles):
                span = slice(t * LANES, (t + 1) * LANES)
                total[k, plain(j), span] = (
                    pair[k, plain(j), span] + pair_in[k, plain(j), span]
                ) * mask[core, t, block(k * per_chunk + j)]

        send_total(k).start()
        store_total(k).start()

    @pl.loop(0, chunks)
    def _(k):
        send_part(k).wait_send()
        send_pair(k).wait_send()
        send_total(k).wait()
        store_total(k).wait()

    for copy in sides + gathers + rims:
        copy.wait_send()


def per_device(perturb, control, diffusivity, sea_mask, fold_partner):
    members, levels, rows, cols = control.shape
    fields = members * levels
    chunks = rows // CHUNK
    span = cols // LANES + 1
    tall = rows + 8 * (PAD + TAIL)
    items = fields + 1 + levels
    count = lax.axis_size("lon")
    f32 = jnp.float32
    any_spec = pl.BlockSpec(memory_space=pl.ANY)
    chunk_buf = pltpu.VMEM((chunks, CHUNK, cols), f32)
    full = pltpu.VMEM((fields, span, tall, LANES), f32)
    by_level = pltpu.VMEM((levels, span, tall, LANES), f32)
    packed = pltpu.VMEM((2, rows // 4, 128), f32)
    dma = pltpu.SemaphoreType.DMA
    return pl.pallas_call(
        kernel,
        out_shape=jax.ShapeDtypeStruct((levels, rows, cols), f32),
        in_specs=[any_spec] * 4 + [pl.BlockSpec(memory_space=pltpu.SMEM)],
        out_specs=any_spec,
        scratch_shapes=[
            full, full, full,
            pltpu.VMEM((fields, rows, cols), f32),
            pltpu.VMEM((span, tall, LANES), f32),
            by_level,
            pltpu.VMEM((levels, rows, cols), jnp.int32),
            by_level, by_level, by_level, by_level,
            packed, packed,
            pltpu.VMEM((items, 8, cols), f32),
            pltpu.VMEM((count - 1, items, 8, cols), f32),
            chunk_buf, chunk_buf, chunk_buf, chunk_buf, chunk_buf,
            dma((2 * span,)), dma((4,)), dma((4,)), dma((3,)), dma((3,)),
            dma((count - 1,)), dma((count - 1,)),
            dma((chunks,)), dma((chunks,)), dma((chunks,)), dma((chunks,)),
            dma((chunks,)), dma((chunks,)), dma((chunks,)),
        ],
        compiler_params=pltpu.CompilerParams(
            collective_id=0, has_side_effects=True, vmem_limit_bytes=60 * 1024 * 1024
        ),
        cost_estimate=pl.CostEstimate(
            flops=40 * fields * rows * cols, bytes_accessed=16 * fields * rows * cols, transcendentals=0
        ),
    )(
        control.reshape(fields, rows, cols),
        perturb.reshape(fields, rows, cols),
        diffusivity,
        sea_mask,
        fold_partner,
    )


def solution(mesh):
    return jax.shard_map(
        per_device,
        mesh=mesh,
        in_specs=(
            P("mem", None, "lat", "lon"),
            P("mem", None, "lat", "lon"),
            P("lat", "lon"),
            P(None, "lat", "lon"),
            P(),
        ),
        out_specs=P(None, "lat", "lon"),
        check_vma=False,
    )
```
